512 devices in a mesh: head: 8 (over x_lo, y), ctx: 64 (over x_hi, z, core).
Axes of the slice: x: 4 (x_hi: 2, x_lo: 2; x = x_hi * 2 + x_lo), y: 4, z: 16, core: 2. Of those that a mesh axis runs over, the one named last changes fastest.
Arguments:
- query_vectors: bfloat16 [8192, 4096], P('ctx', 'head'), may hold values from -120 to 120
- key_vectors: bfloat16 [8192, 1024], P('ctx', 'head'), may hold values from -8 to 8
- value_vectors: bfloat16 [8192, 1024], P('ctx', 'head'), may hold values from -6 to 6
- output_grad: bfloat16 [8192, 4096], P('ctx', 'head'), may hold values from -6 to 6
- out_weight: bfloat16 [4096, 4096], P('head', 'ctx'), may hold values from -0.09375 to 0.09375
- selected: int32 [8, 64, 3], P('head', 'ctx'), may hold values from 0 to 62, as said below
- counts: int32 [8, 64], P('head', 'ctx'), may hold values from 0 to 3, as said below
Outputs:
- query_grad: bfloat16 [8192, 4096], P('ctx', 'head')
- key_grad: bfloat16 [8192, 1024], P('ctx', 'head')
- value_grad: bfloat16 [8192, 1024], P('ctx', 'head')
The draws below stay inside these ranges and needn't reach their ends.
Inputs may be any that keep to these rules, and one draw needn't show every extreme that they name: For block i >= 1, selected[g, i, 0] = i - 1 and the first min(3, i) entries are distinct blocks below i; further entries are 0. counts[g, i] <= min(3, i); the last block has 3 in every head group.
All inputs are finite; a program needn't handle non-finite values.
Results may differ from the reference program's by a relative error of at most 0.0075.
Values may be sent and summed in bfloat16 or wider, within the bound.
A program may use at most 64 MiB of HBM per device.

```python
import jax
import jax.numpy as jnp
from jax import lax

D = 4096
HEADS = 32
KV_HEADS = 8
DH = 128
TOK_DEV = 128
TOPK = 3
NBLOCKS = 64
TOKENS = 8192


def shared_keys(key):
    base = jnp.clip(jax.random.normal(key, (TOKENS, KV_HEADS * DH), jnp.float32), -6.0, 6.0)
    before_last = (jnp.arange(TOKENS) % TOK_DEV == TOK_DEV - 2)[:, None]
    return jnp.where(before_last, base, base)


def draw_key_vectors(key, part):
    return shared_keys(key).astype(jnp.bfloat16)


def draw_query_vectors(key, part):
    own_key = jax.random.fold_in(key, 7)
    entries = jnp.clip(jax.random.normal(own_key, (TOKENS, HEADS * DH), jnp.float32), -6.0, 6.0)
    result = entries
    return result.astype(jnp.bfloat16)


def draw_selected(key, part):
    key = jax.random.fold_in(key, 11)
    noise = jax.random.randint(jax.random.fold_in(key, 1), (KV_HEADS, NBLOCKS, NBLOCKS), 0, 1024)
    liking = jax.random.randint(jax.random.fold_in(key, 2), (KV_HEADS, 1, NBLOCKS), 0, 4)
    blocks = jnp.arange(NBLOCKS, dtype=jnp.int32)
    row_block = blocks[None, :, None]
    col_block = blocks[None, None, :]
    ranking = (noise + 1024 * liking) * NBLOCKS + col_block
    ranking = jnp.where(col_block == row_block - 1, 2 ** 30, ranking)
    ranking = jnp.where(col_block < row_block, ranking, -1 - col_block)
    ranked_values, picked = jax.lax.top_k(ranking, TOPK)
    slot_number = jnp.arange(TOPK, dtype=jnp.int32)[None, None, :]
    picked = jnp.where(slot_number < jnp.minimum(row_block, TOPK), picked, 0)
    return picked.astype(jnp.int32)


def draw_counts(key, part):
    key = jax.random.fold_in(key, 13)
    drawn = jax.random.randint(key, (KV_HEADS, NBLOCKS), 1, TOPK + 1)
    blocks = jnp.arange(NBLOCKS, dtype=jnp.int32)[None, :]
    drawn = jnp.minimum(drawn, blocks)
    drawn = jnp.where(blocks == NBLOCKS - 1, TOPK, drawn)
    return drawn.astype(jnp.int32)


def level_of(key, extent, pieces, smallest, largest):
    def one(dim, shards_of):
        steps = jax.random.uniform(jax.random.fold_in(jax.random.fold_in(key, 6), dim), (shards_of,), jnp.float32, smallest / len(pieces), largest / len(pieces))
        return jnp.repeat(jnp.exp(steps), extent[dim] // shards_of).reshape((-1,) + (1,) * (len(extent) - dim - 1))

    loudness = one(*pieces[0])
    for cut in pieces[1:]:
        loudness = loudness * one(*cut)
    return loudness


def gaussian(key, extent, spread, reach, pieces=(), kind=jnp.bfloat16):
    gain = level_of(key, extent, pieces, -0.22, 0.18) if pieces else 1.0
    array = jax.random.normal(key, extent, jnp.float32) * spread * gain
    return jnp.minimum(jnp.maximum(array, -reach), reach).astype(kind)


def setup_inputs(seed: int = 0) -> dict:
    key_list = jax.random.split(jax.random.key(seed), 8)
    return {
        "query_vectors": draw_query_vectors(jax.random.fold_in(key_list[7], 71), 0),
        "key_vectors": draw_key_vectors(jax.random.fold_in(key_list[7], 71), 0),
        "value_vectors": gaussian(key_list[2], (TOKENS, KV_HEADS * DH), 1.0, 6.0, ((0, 64), (1, 8))),
        "output_grad": gaussian(key_list[3], (TOKENS, D), 1.0, 6.0, ((0, 64), (1, 8))),
        "out_weight": gaussian(key_list[4], (HEADS * DH, D), D ** -0.5, 0.09375, ((0, 8), (1, 64))),
        "selected": draw_selected(jax.random.fold_in(key_list[7], 71), 0),
        "counts": draw_counts(jax.random.fold_in(key_list[7], 71), 0),
    }


def build_mask(slot_valid, block_rows):
    positions = jnp.arange(block_rows, dtype=jnp.int32)
    causal = positions[None, :] <= positions[:, None]
    groups, slot_count = slot_valid.shape
    own_part = jnp.broadcast_to(causal[None], (groups, block_rows, block_rows))
    far_part = jnp.broadcast_to(slot_valid[:, :, None], (groups, slot_count, block_rows))
    far_part = far_part.reshape(groups, 1, slot_count * block_rows)
    far_part = jnp.broadcast_to(far_part, (groups, block_rows, slot_count * block_rows))
    return jnp.concatenate([own_part, far_part], axis=2)


def block_backward(query_blk, key_all, value_all, grad_blk, slot_valid):
    block_rows = query_blk.shape[0]
    softmax_scale = query_blk.shape[-1] ** -0.5
    scores = jnp.einsum('tgrd,gkd->grtk', query_blk, key_all) * softmax_scale
    key_mask = build_mask(slot_valid, block_rows)[:, None]
    masked = jnp.where(key_mask, scores, -jnp.inf)
    row_top = jnp.max(masked, axis=-1, keepdims=True)
    log_total = row_top + jnp.log(jnp.sum(jnp.exp(masked - row_top), axis=-1, keepdims=True))
    attn_probs = jnp.exp(masked - log_total)
    probs_low = lax.optimization_barrier(attn_probs.astype(jnp.bfloat16)).astype(jnp.float32)
    outputs = jnp.einsum('grtk,gkd->tgrd', probs_low, value_all)
    delta_rows = jnp.sum(grad_blk * outputs, axis=-1).transpose(1, 2, 0)[..., None]
    grad_probs = jnp.einsum('tgrd,gkd->grtk', grad_blk, value_all)
    grad_scores = attn_probs * (grad_probs - delta_rows)
    scores_low = lax.optimization_barrier(grad_scores.astype(jnp.bfloat16)).astype(jnp.float32)
    query_part = (jnp.einsum('grtk,gkd->tgrd', scores_low, key_all) * softmax_scale).astype(jnp.bfloat16)
    value_part = jnp.einsum('grtk,tgrd->gkd', probs_low, grad_blk)
    key_part = jnp.einsum('grtk,tgrd->gkd', scores_low, query_blk) * softmax_scale
    return query_part, key_part, value_part


def reference(query_vectors, key_vectors, value_vectors, output_grad, out_weight, selected, counts):
    head_grad = jnp.dot(output_grad, out_weight.T, preferred_element_type=jnp.float32).astype(jnp.bfloat16)
    group_size = HEADS // KV_HEADS
    query_blocks = query_vectors.reshape(NBLOCKS, TOK_DEV, KV_HEADS, group_size, DH)
    grad_blocks = head_grad.reshape(NBLOCKS, TOK_DEV, KV_HEADS, group_size, DH)
    key_source = key_vectors.reshape(NBLOCKS, TOK_DEV, KV_HEADS, DH).transpose(2, 0, 1, 3)
    value_source = value_vectors.reshape(NBLOCKS, TOK_DEV, KV_HEADS, DH).transpose(2, 0, 1, 3)
    take_rows = jax.vmap(lambda source, picked: jnp.take(source, picked, axis=0))

    def per_block(block_index):
        chosen = selected[:, block_index, :]
        slot_live = jnp.arange(TOPK, dtype=jnp.int32)[None, :] < counts[:, block_index][:, None]
        key_far = take_rows(key_source, chosen)
        value_far = take_rows(value_source, chosen)
        key_all = jnp.concatenate([key_source[:, block_index][:, None], key_far], axis=1)
        value_all = jnp.concatenate([value_source[:, block_index][:, None], value_far], axis=1)
        key_all = key_all.reshape(KV_HEADS, -1, DH).astype(jnp.float32)
        value_all = value_all.reshape(KV_HEADS, -1, DH).astype(jnp.float32)
        return block_backward(query_blocks[block_index].astype(jnp.float32), key_all, value_all,
                              grad_blocks[block_index].astype(jnp.float32), slot_live)

    query_part, key_part, value_part = lax.map(per_block, jnp.arange(NBLOCKS, dtype=jnp.int32))
    targets = selected.transpose(1, 0, 2)
    group_index = jnp.broadcast_to(jnp.arange(KV_HEADS, dtype=jnp.int32)[None, :, None], targets.shape)

    def collect(block_parts):
        block_parts = block_parts.reshape(NBLOCKS, KV_HEADS, TOPK + 1, TOK_DEV, DH)
        totals = block_parts[:, :, 0].transpose(1, 0, 2, 3)
        totals = totals.at[group_index, targets].add(block_parts[:, :, 1:])
        return totals.transpose(1, 2, 0, 3).reshape(TOKENS, KV_HEADS * DH).astype(jnp.bfloat16)

    return (query_part.reshape(TOKENS, HEADS * DH), collect(key_part), collect(value_part))
```

```python
import functools

import jax
import jax.numpy as jnp
from jax import lax
from jax.experimental import pallas as pl
from jax.experimental.pallas import tpu as pltpu
from jax.sharding import PartitionSpec as P

MESH = pl.DeviceIdType.MESH
DH = 128
NEG = -1e30
AG_K = 1
RS_K = 2
F32 = jnp.float32
BF16 = jnp.bfloat16


def dot(a, b, dims):
    return lax.dot_general(a, b, (dims, ((), ())), preferred_element_type=F32)


NN = ((1,), (0,))
NT = ((1,), (1,))


def kernel(
    ny, nz,
    q_ref, k_ref, v_ref, og_ref, w_ref, sel_ref, cnt_ref,
    dq_ref, dk_ref, dv_ref,
    kvbuf, wbuf, ogbuf, stage, tiles, ids, csend, crecv,
    kall, vall, pfull, plow, dslow, do4, q4, own_sum, pslot, s0buf, s0r, sbuf, rbuf,
    kv_s, kv_r, kvc_s, kvc_r, w_s, w_r, wc_s, wc_r, ogx_s, ogx_r, ogy_s, ogy_r,
    tile_s, tile_r, ids_s, kvx_s, kvx_r, c_s, c_r, sl_s, sl_r, s0_s, s0_r, rs_s, rs_r,
):
    lane = 2 * nz
    head, ctx = lax.axis_index("head"), lax.axis_index("ctx")
    xl, y = head // ny, head % ny
    xh, z, c = ctx // lane, (ctx // 2) % nz, ctx % 2
    rows = q_ref.shape[0]
    width = q_ref.shape[1]
    heads = width // DH
    half = [nz // 2, nz // 2 - 1]

    def zdev(step):
        return (head, xh * lane + ((z + step + nz) % nz) * 2 + c)

    core_dev = (head, xh * lane + z * 2 + (1 - c))
    x_dev = (head, (1 - xh) * lane + z * 2 + c)
    xc_dev = (head, (1 - xh) * lane + z * 2 + (1 - c))
    prev_dev = (head, (ctx + 2 * lane - 1) % (2 * lane))
    next_dev = (head, (ctx + 1) % (2 * lane))

    def remote(src, dst, send, recv, dev):
        return pltpu.make_async_remote_copy(
            src_ref=src, dst_ref=dst, send_sem=send, recv_sem=recv, device_id=dev, device_id_type=MESH
        )

    barrier = pltpu.get_barrier_semaphore()
    greet = [core_dev, x_dev, xc_dev, prev_dev, next_dev]
    greet += [((1 - xl) * ny + y, ctx), ((1 - xl) * ny + y, (1 - xh) * lane + z * 2 + c)]
    greet += [(xl * ny + (y + dy) % ny, ctx) for dy in range(1, ny)]
    greet += [zdev(sg * k) for k in range(1, max(AG_K, RS_K) + 1) for sg in (1, -1)]
    for dev in greet:
        pl.semaphore_signal(barrier, inc=1, device_id=dev, device_id_type=MESH)

    me = z * 2 + c
    kvbuf[me, 0:rows] = k_ref[...]
    kvbuf[me, rows : 2 * rows] = v_ref[...]
    row_id = lax.broadcasted_iota(jnp.int32, (8, 128), 0)
    tiles[0] = jnp.where(row_id == 0, sel_ref[0, 0, 1], sel_ref[0, 0, 2])
    pl.semaphore_wait(barrier, len(greet))

    def ring(buf, send, recv, dr, off, k):
        sg = 1 if dr == 0 else -1
        slot = ((z - sg * off + nz) % nz) * 2 + c
        return remote(
            buf.at[slot], buf.at[slot], send.at[dr, off + k - 1], recv.at[dr, off + k - 1], zdev(sg * k)
        )

    def to_core(buf, send, recv, slot_z):
        slot = slot_z * 2 + c
        return remote(buf.at[slot], buf.at[slot], send.at[slot_z], recv.at[slot_z], core_dev)

    started = []

    def relay(buf, sems, dr, off):
        send, recv, csnd, crcv = sems
        for k in range(AG_K, 0, -1):
            if off + k <= half[dr]:
                cp = ring(buf, send, recv, dr, off, k)
                cp.start()
                started.append(cp)
        if not (off == 0 and dr == 1):
            sg = 1 if dr == 0 else -1
            cp = to_core(buf, csnd, crcv, (z - sg * off + nz) % nz)
            cp.start()
            started.append(cp)

    def arrived(buf, sems, dr, off):
        ring(buf, sems[0], sems[1], dr, off - 1, 1).wait_recv()

    kv_sems = (kv_s, kv_r, kvc_s, kvc_r)
    w_sems = (w_s, w_r, wc_s, wc_r)
    relay(kvbuf, kv_sems, 0, 0)
    relay(kvbuf, kv_sems, 1, 0)
    wbuf[me] = w_ref[...].T
    relay(wbuf, w_sems, 0, 0)
    relay(wbuf, w_sems, 1, 0)

    tile_cps = [
        remote(tiles.at[0], tiles.at[n], tile_s.at[n - 1], tile_r.at[n - 1], dev)
        for n, dev in ((1, core_dev), (2, x_dev), (3, xc_dev))
    ]
    for cp in tile_cps:
        cp.start()

    ogx = [
        remote(og_ref, ogbuf.at[xh, y], ogx_s.at[t], ogx_r.at[xh], (t * ny + y, xl * lane + z * 2 + c))
        for t in range(2)
    ]
    for t in range(2):
        @pl.when(jnp.logical_not((xh == xl) & (xl == t)))
        def _():
            ogx[t].start()

    @pl.when(xh == xl)
    def _():
        ogbuf[xh, y] = og_ref[...]

    for h in range(heads):
        q4[h * rows : (h + 1) * rows] = q_ref[:, h * DH : (h + 1) * DH]
    for n in range(4):
        pslot[n, 2] = jnp.zeros(pslot.shape[2:], BF16)

    def ogy(b, dy, slot_y):
        return remote(
            ogbuf.at[b, slot_y], ogbuf.at[b, slot_y], ogy_s.at[b, dy - 1], ogy_r.at[b, dy - 1],
            (xl * ny + (y + dy) % ny, ctx),
        )

    def ogx_done():
        for b in range(2):
            @pl.when(jnp.logical_not((xh == b) & (xl == b)))
            def _():
                remote(og_ref, ogbuf.at[b, y], ogx_s.at[0], ogx_r.at[b], x_dev).wait_recv()
        for b in range(2):
            for dy in range(1, ny):
                ogy(b, dy, y).start()

    for off in range(1, half[0] + 1):
        for buf, sems in ((kvbuf, kv_sems), (wbuf, w_sems)):
            for dr in (0, 1):
                if off <= half[dr]:
                    arrived(buf, sems, dr, off)
                    relay(buf, sems, dr, off)
        if off == 2:
            ogx_done()
        if off == 3:
            for cp in tile_cps:
                cp.wait_recv()
            to_ids = pltpu.make_async_copy(tiles, ids, ids_s)
            to_ids.start()
            to_ids.wait()

    def core_wait(buf, sems):
        for slot_z in range(nz):
            slot = slot_z * 2 + (1 - c)
            remote(buf.at[slot], buf.at[slot], sems[2].at[slot_z], sems[3].at[slot_z], core_dev).wait_recv()

    core_wait(kvbuf, kv_sems)

    kvx = [remote(stage.at[n], kvbuf.at[lane + n], kvx_s.at[n], kvx_r.at[n], x_dev) for n in range(3)]
    first = (z == 0) & (c == 0)

    @pl.when(xh == 0)
    def _():
        for n in (1, 2):
            stage[n] = kvbuf[jnp.clip(ids[2, n - 1, 0], 0, lane - 1)]
            kvx[n].start()

        @pl.when(first)
        def _():
            stage[0] = kvbuf[lane - 1]
            kvx[0].start()

    core_wait(wbuf, w_sems)
    for b in range(2):
        for dy in range(1, ny):
            ogy(b, dy, (y - dy + ny) % ny).wait_recv()

    per = lane // ny

    def project(b):
        total = None
        for part in range(ny):
            weight = wbuf[part * per : (part + 1) * per].reshape(-1, width)
            term = dot(ogbuf[b, part], weight, NN)
            total = term if total is None else total + term
        return total

    csend[...] = project(1 - xh).astype(BF16)
    cx = remote(csend, crecv, c_s, c_r, x_dev)
    cx.start()
    own_part = project(xh)

    @pl.when(xh == 1)
    def _():
        for n in (1, 2):
            kvx[n].wait_recv()

        @pl.when(first)
        def _():
            kvx[0].wait_recv()

    kall[0:rows] = k_ref[...]
    vall[0:rows] = v_ref[...]
    for n in range(3):
        b = sel_ref[0, 0, n]
        near = jnp.clip(b - xh * lane, 0, lane - 1)
        block = kvbuf[jnp.where(b >= xh * lane, near, lane + n)]
        kall[(n + 1) * rows : (n + 2) * rows] = block[0:rows]
        vall[(n + 1) * rows : (n + 2) * rows] = block[rows : 2 * rows]

    scale = DH ** -0.5
    count = cnt_ref[0, 0]
    key_pos = lax.broadcasted_iota(jnp.int32, (rows, rows), 0)
    tok_pos = lax.broadcasted_iota(jnp.int32, (rows, rows), 1)
    for h in range(heads):
        part = dot(kall[...], q_ref[:, h * DH : (h + 1) * DH], NT) * scale
        pieces = [jnp.where(key_pos <= tok_pos, part[0:rows], NEG)]
        for n in range(3):
            pieces.append(part[(n + 1) * rows : (n + 2) * rows] + jnp.where(n < count, 0.0, NEG))
        scores = jnp.concatenate(pieces, axis=0)
        top = jnp.max(scores, axis=0, keepdims=True)
        raised = jnp.exp(scores - top)
        probs = raised * (1.0 / jnp.sum(raised, axis=0, keepdims=True))
        pfull[h] = probs
        plow[:, h * rows : (h + 1) * rows] = probs.astype(BF16)

    cx.wait_recv()
    head_grad = (own_part + crecv[...].astype(F32)).astype(BF16)
    for h in range(heads):
        do4[h * rows : (h + 1) * rows] = head_grad[:, h * DH : (h + 1) * DH]
    for h in range(heads):
        grad_probs = dot(vall[...], do4[h * rows : (h + 1) * rows], NT)
        low = plow[:, h * rows : (h + 1) * rows].astype(F32)
        delta = jnp.sum(low * grad_probs, axis=0, keepdims=True)
        dslow[:, h * rows : (h + 1) * rows] = (pfull[h] * (grad_probs - delta)).astype(BF16)

    dv_all = dot(plow[...], do4[...], NN)
    dk_all = dot(dslow[...], q4[...], NN)
    own_sum[0:rows] = dk_all[0:rows]
    own_sum[rows : 2 * rows] = dv_all[0:rows]
    for n in (1, 2):
        pslot[0, n - 1, 0:rows] = dk_all[(n + 1) * rows : (n + 2) * rows].astype(BF16)
        pslot[0, n - 1, rows : 2 * rows] = dv_all[(n + 1) * rows : (n + 2) * rows].astype(BF16)

    def slots(src, dst, n, dev):
        return remote(
            pslot.at[src, pl.ds(0, 2)], pslot.at[dst, pl.ds(0, 2)], sl_s.at[n], sl_r.at[n], dev
        )

    sl_x = slots(0, 2, 1, x_dev)
    sl_c = slots(0, 1, 0, core_dev)
    sl_f = slots(2, 3, 2, core_dev)

    @pl.when(xh == 1)
    def _():
        sl_x.start()

    sl_c.start()
    s0buf[0:rows] = dk_all[rows : 2 * rows].astype(BF16)
    s0buf[rows : 2 * rows] = dv_all[rows : 2 * rows].astype(BF16)
    s0 = remote(s0buf, s0r, s0_s, s0_r, prev_dev)

    @pl.when(ctx > 0)
    def _():
        s0.start()

    key_t = kall[...].T
    for h in range(heads):
        part = dot(key_t, dslow[:, h * rows : (h + 1) * rows], NN) * scale
        dq_ref[:, h * DH : (h + 1) * DH] = part.T.astype(BF16)

    sl_c.wait_recv()

    @pl.when(xh == 0)
    def _():
        sl_x.wait_recv()
        sl_f.start()
        sl_f.wait_recv()

    wanted = [(sel_ref[0, 0, 1], sel_ref[0, 0, 2])] + [(ids[n, 0, 0], ids[n, 1, 0]) for n in (1, 2, 3)]

    def contribution(slot_z):
        target = xh * lane + slot_z * 2 + c
        total = None
        for n, (one, two) in enumerate(wanted):
            index = jnp.where(one == target, 0, jnp.where(two == target, 1, 2))
            term = pslot[n, index].astype(F32)
            total = term if total is None else total + term
        return total

    def rs_copy(dr, o):
        sg = 1 if dr == 0 else -1
        r = o % RS_K or RS_K
        return remote(sbuf.at[dr, o - 1], rbuf.at[dr, o - 1], rs_s.at[dr, o - 1], rs_r.at[dr, o - 1], zdev(sg * r))

    def rs_collect(total, dr, o):
        for o2 in range(o + 1, min(o + RS_K, half[dr]) + 1):
            rs_copy(dr, o2).wait_recv()
            total = total + rbuf[dr, o2 - 1].astype(F32)
        return total

    def rs_send(dr, o):
        sg = 1 if dr == 0 else -1
        total = contribution((z + sg * o + nz) % nz)
        if o % RS_K == 0:
            total = rs_collect(total, dr, o)
        sbuf[dr, o - 1] = total.astype(BF16)
        rs_copy(dr, o).start()

    order = sorted(
        ((dr, o) for dr in (0, 1) for o in range(1, half[dr] + 1)),
        key=lambda m: (-(m[1] if m[1] % RS_K == 0 else m[1] + RS_K + 0.5), m[0]),
    )
    for dr, o in order:
        rs_send(dr, o)
    total = own_sum[...] + contribution(z)

    @pl.when(ctx < 2 * lane - 1)
    def _():
        s0.wait_recv()

    total = total + jnp.where(ctx < 2 * lane - 1, s0r[...].astype(F32), 0.0)
    for dr in (0, 1):
        total = rs_collect(total, dr, 0)
    dk_ref[...] = (total[0:rows] * scale).astype(BF16)
    dv_ref[...] = total[rows : 2 * rows].astype(BF16)

    for cp in started:
        cp.wait_send()
    for cp in tile_cps:
        cp.wait_send()
    for t in range(2):
        @pl.when(jnp.logical_not((xh == xl) & (xl == t)))
        def _():
            ogx[t].wait_send()
    for b in range(2):
        for dy in range(1, ny):
            ogy(b, dy, y).wait_send()
    cx.wait_send()
    sl_c.wait_send()

    @pl.when(xh == 0)
    def _():
        for n in (1, 2):
            kvx[n].wait_send()

        @pl.when(first)
        def _():
            kvx[0].wait_send()

        sl_f.wait_send()

    @pl.when(xh == 1)
    def _():
        sl_x.wait_send()

    @pl.when(ctx > 0)
    def _():
        s0.wait_send()

    for dr, o in order:
        rs_copy(dr, o).wait_send()


def solution(mesh):
    ny, nz = mesh.shape["head"] // 2, mesh.shape["ctx"] // 4
    lane, hz = 2 * nz, nz // 2

    def body(q, k, v, og, w, sel, cnt):
        rows, width = q.shape
        heads = width // DH
        keys = 4 * rows
        vmem, smem = pl.BlockSpec(memory_space=pltpu.VMEM), pl.BlockSpec(memory_space=pltpu.SMEM)
        dma = pltpu.SemaphoreType.DMA
        scratch = [
            pltpu.VMEM((lane + 3, 2 * rows, DH), BF16),
            pltpu.VMEM((lane, w.shape[1], width), BF16),
            pltpu.VMEM((2, ny, rows, width), BF16),
            pltpu.VMEM((3, 2 * rows, DH), BF16),
            pltpu.VMEM((4, 8, 128), jnp.int32),
            pltpu.SMEM((4, 8, 128), jnp.int32),
            pltpu.VMEM((rows, width), BF16),
            pltpu.VMEM((rows, width), BF16),
            pltpu.VMEM((keys, DH), BF16),
            pltpu.VMEM((keys, DH), BF16),
            pltpu.VMEM((heads, keys, rows), F32),
            pltpu.VMEM((keys, heads * rows), BF16),
            pltpu.VMEM((keys, heads * rows), BF16),
            pltpu.VMEM((heads * rows, DH), BF16),
            pltpu.VMEM((heads * rows, DH), BF16),
            pltpu.VMEM((2 * rows, DH), F32),
            pltpu.VMEM((4, 3, 2 * rows, DH), BF16),
            pltpu.VMEM((2 * rows, DH), BF16),
            pltpu.VMEM((2 * rows, DH), BF16),
            pltpu.VMEM((2, hz, 2 * rows, DH), BF16),
            pltpu.VMEM((2, hz, 2 * rows, DH), BF16),
            dma((2, hz)), dma((2, hz)), dma((nz,)), dma((nz,)),
            dma((2, hz)), dma((2, hz)), dma((nz,)), dma((nz,)),
            dma((2,)), dma((2,)), dma((2, ny - 1)), dma((2, ny - 1)),
            dma((3,)), dma((3,)), dma(()), dma((3,)), dma((3,)),
            dma(()), dma(()), dma((3,)), dma((3,)), dma(()), dma(()),
            dma((2, hz)), dma((2, hz)),
        ]
        return pl.pallas_call(
            functools.partial(kernel, ny, nz),
            out_shape=(
                jax.ShapeDtypeStruct(q.shape, BF16),
                jax.ShapeDtypeStruct(k.shape, BF16),
                jax.ShapeDtypeStruct(v.shape, BF16),
            ),
            in_specs=[vmem] * 5 + [smem] * 2,
            out_specs=(vmem, vmem, vmem),
            scratch_shapes=scratch,
            compiler_params=pltpu.CompilerParams(
                collective_id=0, has_side_effects=True, vmem_limit_bytes=40 << 20
            ),
        )(q, k, v, og, w, sel, cnt)

    placed = P("ctx", "head")
    return jax.shard_map(
        body,
        mesh=mesh,
        in_specs=(placed, placed, placed, placed, P("head", "ctx"), P("head", "ctx", None), P("head", "ctx")),
        out_specs=(placed, placed, placed),
        check_vma=False,
    )
```

```python
import functools

import jax
import jax.numpy as jnp
from jax import lax
from jax.experimental import pallas as pl
from jax.experimental.pallas import tpu as pltpu
from jax.sharding import PartitionSpec as P

MESH = pl.DeviceIdType.MESH
DH = 128
NEG = -1e30
RS_K = 2
OG = (1, 2)
UP = 8
F32 = jnp.float32
BF16 = jnp.bfloat16


def dot(a, b, dims):
    return lax.dot_general(a, b, (dims, ((), ())), preferred_element_type=F32)


NN = ((1,), (0,))
NT = ((1,), (1,))


def kernel(
    ny, nz,
    q_hbm, k_hbm, v_hbm, og_hbm, w_hbm, sel_hbm, cnt_hbm,
    dq_ref, dk_ref, dv_ref,
    q_ref, og_ref, sel_ref, cnt_ref, kvbuf, prev_kv, wbuf, ogbuf, stage, taken, tiles, ids, csend, crecv,
    kall, vall, pfull, plow, dslow, do4, q4, own_sum, pslot_k, pslot_v, s0buf, s0r, sbuf, rbuf, xsend, xrecv,
    in_s, first_s, ring_s, ring_r, share_s, share_r, pk_s, pk_r, ogx_s, ogx_r, ogy_s, ogy_r,
    tile_s, tile_r, ids_s, kvx_s, kvx_r, c_s, c_r, sl_s, sl_r, s0_s, s0_r, rs_s, rs_r, cross_s, cross_r,
):
    lane = 2 * nz
    head, ctx = lax.axis_index("head"), lax.axis_index("ctx")
    xl, y = head // ny, head % ny
    xh, z, c = ctx // lane, (ctx // 2) % nz, ctx % 2
    rows, width = q_ref.shape
    pslot = (pslot_k, pslot_v)
    heads = width // DH
    hops, short, sg = UP, nz - 1 - UP, 2 * c - 1
    longer, mate_longer = c == 1, c == 0

    def at(cx, cz, cc, hd=head):
        return (hd, cx * lane + cz * 2 + cc)

    def zdev(step):
        return at(xh, (z + step + nz) % nz, c)

    def mate(r):
        return at(1 - xh if r & 2 else xh, z, 1 - c if r & 1 else c)

    prev_dev = (head, (ctx + 2 * lane - 1) % (2 * lane))
    next_dev = (head, (ctx + 1) % (2 * lane))
    core_dev = mate(1)

    def remote(src, dst, send, recv, dev):
        return pltpu.make_async_remote_copy(
            src_ref=src, dst_ref=dst, send_sem=send, recv_sem=recv, device_id=dev, device_id_type=MESH
        )

    pending = []

    def go(cp, cond=None):
        pending.append((cond, cp))
        if cond is None:
            cp.start()
        else:
            pl.when(cond)(cp.start)

    me = z * 2 + c
    loads = [
        pltpu.make_async_copy(src, dst, in_s.at[n])
        for n, (src, dst) in enumerate((
            (k_hbm, kvbuf.at[me, 0]), (v_hbm, kvbuf.at[me, 1]), (w_hbm, wbuf.at[me]),
            (og_hbm, og_ref), (sel_hbm, sel_ref), (cnt_hbm, cnt_ref), (q_hbm, q_ref),
        ))
    ]
    barrier = pltpu.get_barrier_semaphore()
    greet = [at(xh, (z + step + nz) % nz, t) for step in (1, -1) for t in (0, 1)]
    greet += [mate(1), mate(2), mate(3), prev_dev, next_dev]
    greet += [zdev(t * n) for n in range(2, RS_K + 1) for t in (1, -1)]
    greet += [((1 - xl) * ny + y, mate(r)[1]) for r in (0, 2)]
    greet += [(xl * ny + (y + dy) % ny, ctx) for dy in range(1, ny)]
    for dev in greet:
        pl.semaphore_signal(barrier, inc=1, device_id=dev, device_id_type=MESH)
    for cp in loads:
        cp.start()
    for cp in loads[:2]:
        cp.wait()
    pl.semaphore_wait(barrier, len(greet))

    half_w = wbuf.shape[1] // 2

    def piece(kind, slot, p):
        return kvbuf.at[slot, p] if kind == 0 else wbuf.at[slot, pl.ds(p * half_w, half_w)]

    def ring(kind, off, ln, p):
        part = piece(kind, ((z - sg * off + nz) % nz) * 2 + ln, p)
        return remote(part, part, ring_s.at[kind, off, ln, p], ring_r.at[kind, off, ln, p], zdev(sg))

    def share(kind, slot_z):
        buf = kvbuf if kind == 0 else wbuf
        part = buf.at[pl.ds(slot_z * 2, 2)]
        return remote(part, part, share_s.at[kind, slot_z], share_r.at[kind, slot_z], core_dev)

    def share_own(kind, core):
        buf = kvbuf if kind == 0 else wbuf
        part = buf.at[z * 2 + core]
        return remote(part, part, share_s.at[kind, z], share_r.at[kind, z], core_dev)

    pieces = [(kind, p) for kind in (0, 1) for p in (0, 1)]
    for kind, p in pieces:
        if (kind, p) == (1, 0):
            loads[2].wait()
        part = piece(kind, me, p)
        for t in (0, 1):
            dev = at(xh, (z + 2 * t - 1 + nz) % nz, t)
            go(remote(part, part, first_s.at[kind, t, p], ring_r.at[kind, 0, c, p], dev))

    pk = remote(kvbuf.at[me], prev_kv, pk_s, pk_r, next_dev)
    go(pk, ctx < 2 * lane - 1)
    for kind in (0, 1):
        go(share_own(kind, c))
    for cp in loads[3:6]:
        cp.wait()

    rel = jnp.where(xh == xl, 0, 1)
    for t in (0, 1):
        cp = remote(og_ref, ogbuf.at[y, rel], ogx_s.at[t], ogx_r.at[rel], at(xl, z, c, t * ny + y))
        go(cp, jnp.logical_not((xh == xl) & (xl == t)))

    row_id = lax.broadcasted_iota(jnp.int32, (8, 128), 0)
    tiles[0] = jnp.where(row_id == 0, sel_ref[0, 0, 1], sel_ref[0, 0, 2])
    tile_cps = [remote(tiles.at[0], tiles.at[r], tile_s.at[r - 1], tile_r.at[r - 1], mate(r)) for r in range(1, 4)]
    for cp in tile_cps:
        go(cp)

    @pl.when(xh == xl)
    def _():
        ogbuf[y, 0] = og_ref[...]

    def ogy(b, dy, slot_y):
        part = ogbuf.at[slot_y, b]
        return remote(part, part, ogy_s.at[b, dy - 1], ogy_r.at[b, dy - 1], (xl * ny + (y + dy) % ny, ctx))

    def when(cond, act):
        if cond is None:
            act()
        else:
            pl.when(cond)(act)

    for off in range(hops):
        here = None if off + 1 <= short else longer
        onward = None if off + 2 <= short else longer
        for kind, p in pieces:
            for ln in (0, 1):
                when(here, ring(kind, off, ln, p).wait_recv)
                if off + 1 < hops:
                    go(ring(kind, off + 1, ln, p), onward)
        for kind in (0, 1):
            go(share(kind, (z - sg * (off + 1) + nz) % nz), here)
        if off == 0:
            loads[6].wait()
            for h in range(heads):
                q4[h * rows : (h + 1) * rows] = q_ref[:, h * DH : (h + 1) * DH]
        if off == 1:
            for n in range(4):
                for kv in (0, 1):
                    pslot[kv][n, 2] = jnp.zeros((rows, DH), BF16)
        for b in (0, 1):
            if off == OG[b]:
                wait = remote(og_ref, ogbuf.at[y, b], ogx_s.at[0], ogx_r.at[b], core_dev).wait_recv
                if b == 0:
                    pl.when(xh != xl)(wait)
                else:
                    wait()
                for dy in range(1, ny):
                    go(ogy(b, dy, y))
        if off == 4:
            for cp in tile_cps:
                cp.wait_recv()
            to_ids = pltpu.make_async_copy(tiles, ids, ids_s)
            to_ids.start()
            to_ids.wait()

    def shared(kind):
        share_own(kind, 1 - c).wait_recv()
        for off in range(hops):
            wait = share(kind, (z + sg * (off + 1) + nz) % nz).wait_recv
            when(None if off + 1 <= short else mate_longer, wait)

    shared(0)

    kvx = []
    for n in (0, 1):
        stage[n] = kvbuf[ids[2, n, 0] % lane]
        kvx.append(remote(stage.at[n], taken.at[n], kvx_s.at[n], kvx_r.at[n], mate(2)))
        go(kvx[n], xh == 0)

    shared(1)
    for b in (0, 1):
        for dy in range(1, ny):
            ogy(b, dy, (y - dy + ny) % ny).wait_recv()

    per = lane // ny

    cols = width // 2

    def project(b, part_col):
        total = None
        for part in range(ny):
            weight = wbuf[part * per : (part + 1) * per, :, part_col * cols : (part_col + 1) * cols].reshape(-1, cols)
            term = dot(ogbuf[part, b], weight, NN)
            total = term if total is None else total + term
        return total

    def cx(n, p):
        part = pl.ds(p * (rows // 2), rows // 2)
        return remote(csend.at[n, part], crecv.at[n, part], c_s.at[n, p], c_r.at[n, p], mate(2))

    for n in (0, 1):
        csend[n] = project(1, n).astype(BF16)
        for p in (0, 1):
            go(cx(n, p))
    own_part = [project(0, n) for n in (0, 1)]

    for cp in kvx:
        pl.when(xh == 1)(cp.wait_recv)
    pl.when(ctx > 0)(pk.wait_recv)

    for n in (0, 1):
        dst = (kall, vall)[n]
        dst[0:rows] = kvbuf[me, n]
        dst[rows : 2 * rows] = prev_kv[n]
    for s in (0, 1):
        b = sel_ref[0, 0, s + 1]
        block = jnp.where(b // lane != xh, taken[s], kvbuf[b % lane])
        kall[(s + 2) * rows : (s + 3) * rows] = block[0]
        vall[(s + 2) * rows : (s + 3) * rows] = block[1]

    scale = DH ** -0.5
    count = cnt_ref[0, 0]

    @pl.when(ctx == 0)
    def _():
        kall[rows : 2 * rows] = jnp.zeros((rows, DH), BF16)
        vall[rows : 2 * rows] = jnp.zeros((rows, DH), BF16)

    key_pos = lax.broadcasted_iota(jnp.int32, (rows, rows), 0)
    tok_pos = lax.broadcasted_iota(jnp.int32, (rows, rows), 1)
    for h in range(heads):
        part = dot(kall[...], q_ref[:, h * DH : (h + 1) * DH], NT) * scale
        parts = [jnp.where(key_pos <= tok_pos, part[0:rows], NEG)]
        for n in range(3):
            parts.append(part[(n + 1) * rows : (n + 2) * rows] + jnp.where(n < count, 0.0, NEG))
        scores = jnp.concatenate(parts, axis=0)
        top = jnp.max(scores, axis=0, keepdims=True)
        raised = jnp.exp(scores - top)
        probs = raised * (1.0 / jnp.sum(raised, axis=0, keepdims=True))
        pfull[h] = probs
        plow[:, h * rows : (h + 1) * rows] = probs.astype(BF16)

    for n in (0, 1):
        for p in (0, 1):
            cx(n, p).wait_recv()
        head_grad = (own_part[n] + crecv[n].astype(F32)).astype(BF16)
        for h in range(heads // 2):
            do4[(n * (heads // 2) + h) * rows : (n * (heads // 2) + h + 1) * rows] = head_grad[:, h * DH : (h + 1) * DH]

    def slots(kv, src, dst, n, dev):
        return [
            remote(pslot[kv].at[src, t], pslot[kv].at[dst, t], sl_s.at[kv, n, t], sl_r.at[kv, n, t], dev)
            for t in (0, 1)
        ]

    def offer(kv, grad):
        own_sum[kv] = grad[0:rows]
        s0buf[kv] = grad[rows : 2 * rows].astype(BF16)
        for s in (0, 1):
            pslot[kv][0, s] = grad[(s + 2) * rows : (s + 3) * rows].astype(BF16)
        for cp in slots(kv, 0, 2, 1, mate(2)):
            go(cp, xh == 1)
        for cp in slots(kv, 0, 1, 0, core_dev):
            go(cp)

    def pass_on(kv):
        for cp, onward in zip(slots(kv, 0, 2, 1, mate(2)), slots(kv, 2, 3, 2, core_dev)):
            pl.when(xh == 0)(cp.wait_recv)
            go(onward, xh == 0)

    def gathered(kv):
        for cp in slots(kv, 0, 1, 0, core_dev):
            cp.wait_recv()
        for cp in slots(kv, 2, 3, 2, core_dev):
            pl.when(xh == 0)(cp.wait_recv)

    offer(1, dot(plow[...], do4[...], NN))
    for h in range(heads):
        grad_probs = dot(vall[...], do4[h * rows : (h + 1) * rows], NT)
        low = plow[:, h * rows : (h + 1) * rows].astype(F32)
        delta = jnp.sum(low * grad_probs, axis=0, keepdims=True)
        dslow[:, h * rows : (h + 1) * rows] = (pfull[h] * (grad_probs - delta)).astype(BF16)
    offer(0, dot(dslow[...], q4[...], NN))
    s0 = remote(s0buf, s0r, s0_s, s0_r, prev_dev)
    go(s0, ctx > 0)
    pass_on(1)

    key_t = kall[...].T
    for h in range(heads):
        part = dot(key_t, dslow[:, h * rows : (h + 1) * rows], NN) * scale
        dq_ref[:, h * DH : (h + 1) * DH] = part.T.astype(BF16)

    wanted = [(sel_ref[0, 0, 1], sel_ref[0, 0, 2])] + [(ids[r, 0, 0], ids[r, 1, 0]) for r in range(1, 4)]

    def contribution(kv, slot_z, ln):
        target = xh * lane + slot_z * 2 + ln
        total = None
        for r, (one, two) in enumerate(wanted):
            index = jnp.where(one == target, 0, jnp.where(two == target, 1, 2))
            term = pslot[kv][r, index].astype(F32)
            total = term if total is None else total + term
        return total

    def rs_copy(kv, o, ln):
        sems = rs_s.at[kv, o - 1, ln], rs_r.at[kv, o - 1, ln]
        dev = zdev(sg * (o % RS_K or RS_K))
        return remote(sbuf.at[kv, o - 1, ln], rbuf.at[kv, o - 1, ln], *sems, dev)

    def rs_collect(total, kv, o, ln):
        for o2 in range(min(o + RS_K, hops), o, -1):
            if o2 <= short:
                rs_copy(kv, o2, ln).wait_recv()
                total = total + rbuf[kv, o2 - 1, ln].astype(F32)
            else:
                pl.when(longer)(rs_copy(kv, o2, ln).wait_recv)
                total = total + jnp.where(longer, rbuf[kv, o2 - 1, ln].astype(F32), 0.0)
        return total

    def rs_send(kv, o):
        for ln in (0, 1):
            total = contribution(kv, (z + sg * o + nz) % nz, ln)
            if o % RS_K == 0:
                total = rs_collect(total, kv, o, ln)
            sbuf[kv, o - 1, ln] = total.astype(BF16)
            go(rs_copy(kv, o, ln), None if o <= short else longer)

    late = [o for p in range(hops - 2, 0, -2) for o in (p - 1, p)]

    gathered(1)
    for o in (hops, hops - 1):
        rs_send(1, o)
    pass_on(0)
    gathered(0)
    for o in (hops, hops - 1):
        rs_send(0, o)
    for o in late:
        for kv in (1, 0):
            rs_send(kv, o)

    pl.when(ctx < 2 * lane - 1)(s0.wait_recv)
    cross = [remote(xsend.at[kv], xrecv.at[kv], cross_s.at[kv], cross_r.at[kv], core_dev) for kv in (0, 1)]
    for kv in (1, 0):
        zero = jnp.zeros((rows, DH), F32)
        ends = [rs_collect(zero, kv, 0, ln) for ln in (0, 1)]
        xsend[kv] = jnp.where(c == 0, ends[1], ends[0]).astype(BF16)
        go(cross[kv])
        total = own_sum[kv] + contribution(kv, z, c) + jnp.where(c == 0, ends[0], ends[1])
        own_sum[kv] = total + jnp.where(ctx < 2 * lane - 1, s0r[kv].astype(F32), 0.0)
    for kv in (1, 0):
        cross[kv].wait_recv()
        total = own_sum[kv] + xrecv[kv].astype(F32)
        if kv == 1:
            dv_ref[...] = total.astype(BF16)
        else:
            dk_ref[...] = (total * scale).astype(BF16)

    for cond, cp in pending:
        if cond is None:
            cp.wait_send()
        else:
            pl.when(cond)(cp.wait_send)


def solution(mesh):
    ny, nz = mesh.shape["head"] // 2, mesh.shape["ctx"] // 4
    lane = 2 * nz

    def body(q, k, v, og, w, sel, cnt):
        rows, width = q.shape
        heads = width // DH
        keys = 4 * rows
        vmem, hbm = pl.BlockSpec(memory_space=pltpu.VMEM), pl.BlockSpec(memory_space=pltpu.HBM)
        dma = pltpu.SemaphoreType.DMA
        scratch = [
            pltpu.VMEM(q.shape, BF16),
            pltpu.VMEM(og.shape, BF16),
            pltpu.SMEM(sel.shape, jnp.int32),
            pltpu.SMEM(cnt.shape, jnp.int32),
            pltpu.VMEM((lane, 2, rows, DH), BF16),
            pltpu.VMEM((2, rows, DH), BF16),
            pltpu.VMEM((lane, w.shape[1], width), BF16),
            pltpu.VMEM((ny, 2, rows, width), BF16),
            pltpu.VMEM((2, 2, rows, DH), BF16),
            pltpu.VMEM((2, 2, rows, DH), BF16),
            pltpu.VMEM((4, 8, 128), jnp.int32),
            pltpu.SMEM((4, 8, 128), jnp.int32),
            pltpu.VMEM((2, rows, width // 2), BF16),
            pltpu.VMEM((2, rows, width // 2), BF16),
            pltpu.VMEM((keys, DH), BF16),
            pltpu.VMEM((keys, DH), BF16),
            pltpu.VMEM((heads, keys, rows), F32),
            pltpu.VMEM((keys, heads * rows), BF16),
            pltpu.VMEM((keys, heads * rows), BF16),
            pltpu.VMEM((heads * rows, DH), BF16),
            pltpu.VMEM((heads * rows, DH), BF16),
            pltpu.VMEM((2, rows, DH), F32),
            pltpu.VMEM((4, 3, rows, DH), BF16),
            pltpu.VMEM((4, 3, rows, DH), BF16),
            pltpu.VMEM((2, rows, DH), BF16),
            pltpu.VMEM((2, rows, DH), BF16),
            pltpu.VMEM((2, UP, 2, rows, DH), BF16),
            pltpu.VMEM((2, UP, 2, rows, DH), BF16),
            pltpu.VMEM((2, rows, DH), BF16),
            pltpu.VMEM((2, rows, DH), BF16),
            dma((7,)),
            dma((2, 2, 2)), dma((2, UP, 2, 2)), dma((2, UP, 2, 2)),
            dma((2, nz)), dma((2, nz)),
            dma(()), dma(()),
            dma((2,)), dma((2,)), dma((2, ny - 1)), dma((2, ny - 1)),
            dma((3,)), dma((3,)), dma(()), dma((2,)), dma((2,)),
            dma((2, 2)), dma((2, 2)), dma((2, 3, 2)), dma((2, 3, 2)), dma(()), dma(()),
            dma((2, UP, 2)), dma((2, UP, 2)), dma((2,)), dma((2,)),
        ]
        return pl.pallas_call(
            functools.partial(kernel, ny, nz),
            out_shape=(
                pltpu.VMEM(q.shape, BF16),
                pltpu.VMEM(k.shape, BF16),
                pltpu.VMEM(v.shape, BF16),
            ),
            in_specs=[hbm] * 7,
            out_specs=(vmem, vmem, vmem),
            scratch_shapes=scratch,
            compiler_params=pltpu.CompilerParams(
                collective_id=0, has_side_effects=True, vmem_limit_bytes=60 << 20
            ),
        )(q, k, v, og, w.T, sel, cnt)

    placed = P("ctx", "head")
    return jax.shard_map(
        body,
        mesh=mesh,
        in_specs=(placed, placed, placed, placed, P("head", "ctx"), P("head", "ctx", None), P("head", "ctx")),
        out_specs=(placed, placed, placed),
        check_vma=False,
    )
```
